256 devices in a mesh: grp: 4 (over x), row: 4 (over y_lo, core), col: 16 (over y_hi, z).
Axes of the slice: x: 4, y: 4 (y_hi: 2, y_lo: 2; y = y_hi * 2 + y_lo), z: 8, core: 2. Of those that a mesh axis runs over, the one named last changes fastest.
Arguments:
- acts: bfloat16 [16, 1024, 4096], P('grp', None, 'row'), may hold values from -6 to 6
- grads: bfloat16 [16, 1024, 4096], P('grp', None, 'col'), may hold values from -6 to 6
- act_basis: bfloat16 [4096, 4096], P('row', 'col'), may hold values from -0.09375 to 0.09375
- grad_basis: bfloat16 [4096, 4096], P('col', ('grp', 'row')), may hold values from -0.09375 to 0.09375
Outputs:
- eigenvalues: float32 [4096, 4096], P(('grp', 'row'), 'col')
The draws below stay inside these ranges and needn't reach their ends.
All inputs are finite; a program needn't handle non-finite values.
Results may differ from the reference program's by a relative error of at most 0.002.
Values may be sent and summed in bfloat16 or wider, within the bound.
A program may use at most 128 MiB of HBM per device.

```python
import jax
import jax.numpy as jnp
from jax import lax

D = 4096
LEN = 1024
SEQS = 16


def raised(entries, own_key, source, target, blocks, factor):
    owner, partner = [(jnp.arange(entries.shape[axis_at]) // (entries.shape[axis_at] // blocks)).reshape([-1 if axis == axis_at else 1 for axis in range(entries.ndim)]) for axis_at in (source, target)]
    chosen = jax.random.permutation(own_key, blocks)[partner]
    strong = (owner == chosen) | (owner == (partner + blocks // 2) % blocks)
    return jnp.where(strong, factor * entries, entries)


def level_of(own_key, shape, shards, low, largest):
    factor_of = 1.0
    for dim, blocks in shards:
        steps = jax.random.uniform(jax.random.fold_in(jax.random.fold_in(own_key, 6), dim), (blocks,), jnp.float32, low / len(shards), largest / len(shards))
        factor_of = factor_of * jnp.repeat(jnp.exp(steps), shape[dim] // blocks).reshape((-1,) + (1,) * (len(shape) - 1 - dim))
    return factor_of


def normal_values(stream_key, extent, spread, reach, pieces=(), kind=jnp.bfloat16):
    factor_of = level_of(stream_key, extent, pieces, -0.22, 0.18) if pieces else 1.0
    entries = jax.random.normal(stream_key, extent, jnp.float32) * spread * factor_of
    return jnp.minimum(jnp.maximum(entries, -reach), reach).astype(kind)


def gaussian_with(own_key, extent, scale, limit, pieces, heavy, dtype=jnp.bfloat16):
    result = scale * jax.random.normal(own_key, extent, jnp.float32)
    if pieces:
        result = result * level_of(own_key, extent, pieces, -0.22, 0.18)
    return jnp.clip(raised(result, jax.random.fold_in(own_key, 3), *heavy), -limit, limit).astype(dtype)


def setup_inputs(seed: int = 0) -> dict:
    arg_keys = jax.random.split(jax.random.key(seed), 5)
    return {
        "acts": normal_values(arg_keys[0], (SEQS, LEN, D), 1.0, 6.0, ((0, 4), (2, 4))),
        "grads": gaussian_with(arg_keys[1], (SEQS, LEN, D), 1.0, 6.0, ((0, 4), (2, 16)), (2, 1, 16, 2.0)),
        "act_basis": normal_values(arg_keys[2], (D, D), D ** -0.5, 0.09375, ((0, 4), (1, 16))),
        "grad_basis": normal_values(arg_keys[3], (D, D), D ** -0.5, 0.09375, ((0, 16), (1, 16))),
    }


def reference(acts, grads, act_basis, grad_basis):
    rotated_grads = jnp.dot(grads.reshape(SEQS * LEN, D), grad_basis, preferred_element_type=jnp.float32).astype(jnp.bfloat16).reshape(SEQS, LEN, D)
    rotated_acts = jnp.dot(acts.reshape(SEQS * LEN, D), act_basis, preferred_element_type=jnp.float32).astype(jnp.bfloat16).reshape(SEQS, LEN, D)

    def accumulate(total, pair):
        grad_seq, act_seq = pair
        tile = jnp.dot(grad_seq.T, act_seq, preferred_element_type=jnp.float32)
        return total + tile * tile, None

    total, unused = lax.scan(accumulate, jnp.zeros((D, D), jnp.float32), (rotated_grads, rotated_acts))
    return total / jnp.float32(SEQS * LEN)
```

```python
import jax
import jax.numpy as jnp
from jax import lax
from jax.experimental import pallas as pl
from jax.experimental.pallas import tpu as pltpu
from jax.sharding import PartitionSpec as P

MESH = pl.DeviceIdType.MESH
F32 = jnp.float32
BF16 = jnp.bfloat16


def kernel(acts, grads, actb, gradb, out, *scratch):
    (gsrc, xs, gq, bas, gp, gs, gr, gt, av, actv, ap, ar, abs_, abr, aown, axs, agat,
     ob, obr, oacc, zsnd, fin,
     ld, xs_s, xs_r, za_s, za_r, xg_s, xg_r, bz_s, bz_r, bb_s, bb_r, kb_s, kb_r, ak_s, ak_r, ab_s, ab_r,
     ax_s, ax_r, az_s, az_r, axg_s, axg_r, h_s, h_r, gt_s, gt_r, ob_s, ob_r, oz_s, oz_r) = scratch
    x = lax.axis_index("grp")
    r = lax.axis_index("row")
    c = lax.axis_index("col")
    b, k, h, z = r // 2, r % 2, c // 8, c % 8
    p = (b + h) % 2
    scale = 1.0 / 16384.0

    def dev(x_, b_, k_, h_, z_):
        return (x_, 2 * b_ + k_, 8 * h_ + z_)

    core_peer = dev(x, b, 1 - k, h, z)
    b_peer = dev(x, 1 - b, k, h, z)
    h_peer = dev(x, 1 - b, k, 1 - h, z)
    xp, xm, x2 = (x + 1) % 4, (x + 3) % 4, (x + 2) % 4
    xp_peer, xm_peer = dev(xp, b, k, h, z), dev(xm, b, k, h, z)
    zp_peer, zm_peer = dev(x, b, k, h, (z + 1) % 8), dev(x, b, k, h, (z + 7) % 8)

    def cp(src, dst, ss, rs, to):
        return pltpu.make_async_remote_copy(
            src_ref=src, dst_ref=dst, send_sem=ss, recv_sem=rs, device_id=to, device_id_type=MESH)

    sent = []

    def send(src, dst, ss, rs, to):
        d = cp(src, dst, ss, rs, to)
        d.start()
        sent.append(d)

    def got(dst, rs):
        cp(dst, dst, ld.at[9], rs, core_peer).wait_recv()

    l_g = pltpu.make_async_copy(grads.at[pl.ds(2 * p, 2), :, k], gsrc, ld.at[0])
    l_x = pltpu.make_async_copy(grads.at[pl.ds(2 * p, 2), x, k], xs.at[x], ld.at[1])
    rb_own = 2 * b + k
    l_b = pltpu.make_async_copy(gradb, bas.at[rb_own, pl.ds(pl.multiple_of(z * 256, 256), 256), :], ld.at[2])
    l_ab = pltpu.make_async_copy(actb, actv, ld.at[3])
    order = (2 * (1 - p) + 1 - k, 2 * (1 - p) + k, 2 * p + 1 - k, 2 * p + k)
    l_a = [pltpu.make_async_copy(acts.at[s], av.at[i], ld.at[4 + i]) for i, s in enumerate(order)]
    for d in [l_g, l_x, l_b, l_ab] + l_a:
        d.start()

    bar = pltpu.get_barrier_semaphore()

    def sig(to):
        pl.semaphore_signal(bar, inc=1, device_id=to, device_id_type=MESH)

    for to in (core_peer, b_peer, h_peer, xp_peer, xm_peer, dev(x2, b, k, h, z)):
        sig(to)

    @pl.loop(1, 8)
    def _(d):
        zt = (z + d) % 8
        sig(dev(x, b, k, h, zt))
        sig(dev(x, b, 1 - k, h, zt))

    pl.semaphore_wait(bar, 20)

    l_g.wait()
    for dx in (1, 3, 2):
        xt = (x + dx) % 4
        send(gsrc.at[:, xt], xs.at[x], xs_s.at[dx], xs_r.at[dx], dev(xt, b, k, h, z))

    def unit(rb, zs):
        return bas.at[rb, pl.ds(pl.multiple_of(zs * 256, 256), 256), :]

    def half(rb, zs, i):
        return bas.at[rb, pl.ds(pl.multiple_of(zs * 256 + 128 * i, 128), 128), :]

    rb_other = 2 * (1 - b) + k

    def b_send(zs):
        send(unit(rb_own, zs), unit(rb_own, zs), bb_s.at[zs], bb_r.at[zs], b_peer)

    l_b.wait()
    send(unit(rb_own, z), unit(rb_own, z), bz_s.at[0, 0], bz_r.at[0, 0], zp_peer)
    send(unit(rb_own, z), unit(rb_own, z), bz_s.at[1, 0], bz_r.at[1, 0], zm_peer)
    b_send(z)

    def ring(d):
        fwd, bwd = (z - d + 8) % 8, (z + d) % 8
        if d < 3:
            got(unit(rb_own, fwd), bz_r.at[0, d - 1])
            send(unit(rb_own, fwd), unit(rb_own, fwd), bz_s.at[0, d], bz_r.at[0, d], zp_peer)
            got(unit(rb_own, bwd), bz_r.at[1, d - 1])
            send(unit(rb_own, bwd), unit(rb_own, bwd), bz_s.at[1, d], bz_r.at[1, d], zm_peer)
            b_send(fwd)
            b_send(bwd)
        elif d == 3:
            got(unit(rb_own, fwd), bz_r.at[0, 2])
            send(half(rb_own, fwd, 0), half(rb_own, fwd, 0), bz_s.at[0, 3], bz_r.at[0, 3], zp_peer)
            got(unit(rb_own, bwd), bz_r.at[1, 2])
            send(half(rb_own, bwd, 1), half(rb_own, bwd, 1), bz_s.at[1, 3], bz_r.at[1, 3], zm_peer)
            b_send(fwd)
            b_send(bwd)
        else:
            got(half(rb_own, fwd, 0), bz_r.at[0, 3])
            got(half(rb_own, fwd, 1), bz_r.at[1, 3])
            b_send(fwd)
            send(bas.at[rb_own], bas.at[rb_own], kb_s.at[0], kb_r.at[0], core_peer)

    def a_part(i):
        l_a[i].wait()

        @pl.loop(0, 4)
        def _(m):
            rows = pl.ds(pl.multiple_of(m * 256, 256), 256)
            ap[i, rows, :] = jnp.dot(av[i, rows, :], actv[...], preferred_element_type=F32)

    l_ab.wait()
    a_part(0)
    send(ap.at[0], ar.at[0], ak_s.at[0], ak_r.at[0], core_peer)

    l_x.wait()
    for dx in (1, 3, 2):
        got(xs.at[(x + 4 - dx) % 4], xs_r.at[dx])
    lane = pl.ds(pl.multiple_of(z * 256, 256), 256)

    @pl.loop(1, 8)
    def _(d):
        zt = (z + d) % 8
        cp(xs.at[zt // 2, zt % 2], gq.at[x, :, lane], za_s.at[d], za_r.at[d], dev(x, b, k, h, zt)).start()

    gq[x, :, lane] = xs[z // 2, z % 2]

    ring(1)
    a_part(1)
    got(ar.at[0], ak_r.at[0])

    @pl.loop(0, 4)
    def _(m):
        rows = pl.ds(pl.multiple_of(m * 256, 256), 256)
        abs_[rows, :] = (ap[1, rows, :] + ar[0, rows, :]).astype(BF16)

    send(abs_, abr, ab_s, ab_r, b_peer)
    ring(2)
    a_part(2)
    send(ap.at[2], ar.at[1], ak_s.at[1], ak_r.at[1], core_peer)
    ring(3)
    a_part(3)
    ring(4)

    @pl.loop(1, 8)
    def _(d):
        zs = (z + 8 - d) % 8
        got(gq.at[x, :, pl.ds(pl.multiple_of(zs * 256, 256), 256)], za_r.at[d])

    def gh(q, i):
        return gq.at[q, pl.ds(64 * i, 64), :]

    for i, j, to in ((0, 0, xp_peer), (3, 1, xm_peer), (1, 1, xp_peer), (4, 0, xm_peer)):
        send(gh(x, j), gh(x, j), xg_s.at[i], xg_r.at[i], to)

    got(ar.at[1], ak_r.at[1])
    got(abr, ab_r)

    @pl.loop(0, 4)
    def _(m):
        rows = pl.ds(pl.multiple_of(m * 256, 256), 256)
        aown[m] = (ap[3, rows, :] + ar[1, rows, :] + abr[rows, :].astype(F32)).astype(BF16)

    for dx in (1, 3, 2):
        xt = (x + dx) % 4
        send(aown.at[xt], axs.at[x], ax_s.at[dx], ax_r.at[dx], dev(xt, b, k, h, z))
    axs[x] = aown[x]
    for dx in (1, 3, 2):
        got(axs.at[(x + 4 - dx) % 4], ax_r.at[dx])
    quarter = pl.ds(pl.multiple_of(x * 256, 256), 256)

    def az(e):
        return cp(axs.at[e], agat.at[z // 2, quarter, :], az_s.at[e], az_r.at[z // 2], dev(x, b, z % 2, h, 2 * e + k))

    for e in range(4):
        @pl.when(2 * e + k != z)
        def _():
            az(e).start()

        @pl.when(2 * e + k == z)
        def _():
            agat[z // 2, quarter, :] = axs[e]

    @pl.loop(0, 8)
    def _(zs):
        got(unit(rb_other, zs), bb_r.at[zs])

    send(bas.at[rb_other], bas.at[rb_other], kb_s.at[1], kb_r.at[1], core_peer)
    got(bas.at[2 * b + 1 - k], kb_r.at[0])
    got(bas.at[2 * (1 - b) + 1 - k], kb_r.at[1])

    def g_part(qi, q):
        for i, bb in enumerate((b, 1 - b)):
            for kk in range(2):
                rb = 2 * bb + kk
                part = jnp.dot(gq[q], bas[rb], preferred_element_type=F32)
                gp[q, rb] = part
                gs[q, rb] = part.astype(BF16)
            pair = pl.ds(2 * bb, 2)
            send(gs.at[q, pair], gr.at[q, pair], h_s.at[qi, i], h_r.at[qi, i], h_peer)

    g_part(0, x)
    got(gh(xm, 0), xg_r.at[0])
    send(gh(xm, 0), gh(xm, 0), xg_s.at[2], xg_r.at[2], xp_peer)
    got(gh(xp, 1), xg_r.at[3])
    send(gh(xp, 1), gh(xp, 1), xg_s.at[5], xg_r.at[5], xm_peer)

    for u in range(4):
        @pl.when(2 * u + k != z)
        def _():
            got(agat.at[u, quarter, :], az_r.at[u])

    def ah(q, j):
        return agat.at[pl.ds(2 * j, 2), pl.ds(pl.multiple_of(q * 256, 256), 256), :]

    for i, j, to in ((0, 0, xp_peer), (3, 1, xm_peer), (1, 1, xp_peer), (4, 0, xm_peer)):
        send(ah(x, j), ah(x, j), axg_s.at[i], axg_r.at[i], to)

    got(gh(xm, 1), xg_r.at[1])
    g_part(1, xm)
    got(gh(xp, 0), xg_r.at[4])
    g_part(2, xp)
    got(gh(x2, 0), xg_r.at[2])
    got(gh(x2, 1), xg_r.at[5])
    g_part(3, x2)

    got(ah(xm, 0), axg_r.at[0])
    send(ah(xm, 0), ah(xm, 0), axg_s.at[2], axg_r.at[2], xp_peer)
    got(ah(xp, 1), axg_r.at[3])
    send(ah(xp, 1), ah(xp, 1), axg_s.at[5], axg_r.at[5], xm_peer)

    def tok(q, kk):
        return pl.ds(pl.multiple_of(q * 256 + kk * 128, 128), 128)

    def g_done(qi, q):
        for i, bb in enumerate((1 - b, b)):
            pair = pl.ds(2 * bb, 2)
            got(gr.at[q, pair], h_r.at[qi, i])
            for kk in range(2):
                rb = 2 * bb + kk
                g = (gp[q, rb] + gr[q, rb].astype(F32)).astype(BF16)
                gt[rb, :, tok(q, k)] = g.T
        send(gt.at[:, :, tok(q, k)], gt.at[:, :, tok(q, k)], gt_s.at[qi], gt_r.at[qi], core_peer)

    for qi, q in enumerate((x, xm, xp, x2)):
        g_done(qi, q)
    for qi, q in enumerate((x, xm, xp, x2)):
        got(gt.at[:, :, tok(q, 1 - k)], gt_r.at[qi])

    got(ah(xm, 1), axg_r.at[1])
    got(ah(xp, 0), axg_r.at[4])
    got(ah(x2, 0), axg_r.at[2])
    got(ah(x2, 1), axg_r.at[5])

    def tile(rb, u):
        t = jnp.dot(gt[rb], agat[u], preferred_element_type=F32)
        return t * t * scale

    for u in range(4):
        for kk in range(2):
            ob[u, kk] = tile(2 * (1 - b) + kk, u).astype(BF16)
        send(ob.at[u], obr.at[u], ob_s.at[u], ob_r.at[u], b_peer)

    def oz(u, kk):
        return cp(zsnd.at[u, kk], fin.at[z], oz_s.at[u, kk], oz_r.at[z], dev(x, b, kk, h, 2 * u + k))

    def here(u, kk):
        return jnp.logical_and(2 * u + k == z, kk == k)

    for u in range(4):
        for kk in range(2):
            oacc[kk] = tile(2 * b + kk, u)
        got(obr.at[u], ob_r.at[u])
        for kk in range(2):
            v = (oacc[kk] + obr[u, kk].astype(F32)).astype(BF16)
            zsnd[u, kk] = v

            @pl.when(jnp.logical_not(here(u, kk)))
            def _():
                oz(u, kk).start()

            @pl.when(here(u, kk))
            def _():
                fin[z] = zsnd[u, kk]

    @pl.loop(0, 8)
    def _(zs):
        @pl.when(jnp.logical_not(jnp.logical_and(zs == z, z % 2 == k)))
        def _():
            got(fin.at[zs], oz_r.at[zs])

    total = fin[0].astype(F32)
    for i in range(1, 8):
        total = total + fin[i].astype(F32)
    out[...] = total

    for d in sent:
        d.wait_send()

    @pl.loop(1, 8)
    def _(d):
        zt = (z + d) % 8
        cp(xs.at[zt // 2, zt % 2], gq.at[x, :, lane], za_s.at[d], za_r.at[d], dev(x, b, k, h, zt)).wait_send()

    for e in range(4):
        @pl.when(2 * e + k != z)
        def _():
            az(e).wait_send()

    for u in range(4):
        for kk in range(2):
            @pl.when(jnp.logical_not(here(u, kk)))
            def _():
                oz(u, kk).wait_send()


def per_device(acts, grads, act_basis, grad_basis):
    grads = grads.reshape(4, 4, 2, 128, 256)
    V = pltpu.VMEM
    DMA = pltpu.SemaphoreType.DMA
    buffers = [
        V((2, 4, 128, 256), BF16), V((4, 2, 128, 256), BF16), V((4, 128, 2048), BF16), V((4, 2048, 256), BF16),
        V((4, 4, 128, 256), F32), V((4, 4, 128, 256), BF16), V((4, 4, 128, 256), BF16), V((4, 256, 1024), BF16),
        V((4, 1024, 1024), BF16), V((1024, 256), BF16), V((4, 1024, 256), F32), V((2, 1024, 256), F32),
        V((1024, 256), BF16), V((1024, 256), BF16), V((4, 256, 256), BF16), V((4, 256, 256), BF16),
        V((4, 1024, 256), BF16),
        V((4, 2, 256, 256), BF16), V((4, 2, 256, 256), BF16), V((2, 256, 256), F32), V((4, 2, 256, 256), BF16),
        V((8, 256, 256), BF16),
    ]
    sems = [DMA((10,)), DMA((4,)), DMA((4,)), DMA((8,)), DMA((8,)), DMA((6,)), DMA((6,)), DMA((2, 4)), DMA((2, 4)),
            DMA((8,)), DMA((8,)), DMA((2,)), DMA((2,)), DMA((2,)), DMA((2,)), DMA, DMA,
            DMA((4,)), DMA((4,)), DMA((4,)), DMA((4,)), DMA((6,)), DMA((6,)), DMA((4, 2)), DMA((4, 2)),
            DMA((4,)), DMA((4,)), DMA((4,)), DMA((4,)), DMA((4, 2)), DMA((8,))]
    hbm = pl.BlockSpec(memory_space=pl.ANY)
    return pl.pallas_call(
        kernel,
        out_shape=jax.ShapeDtypeStruct((256, 256), F32),
        in_specs=[hbm] * 4,
        out_specs=pl.BlockSpec(memory_space=pltpu.VMEM),
        scratch_shapes=buffers + sems,
        compiler_params=pltpu.CompilerParams(
            collective_id=0, has_side_effects=True, vmem_limit_bytes=56 * 2**20),
        cost_estimate=pl.CostEstimate(flops=6442450944, bytes_accessed=11534336, transcendentals=0),
    )(acts, grads, act_basis, grad_basis)


def solution(mesh):
    placed = (
        P("grp", None, "row"),
        P("grp", None, "col"),
        P("row", "col"),
        P("col", ("grp", "row")),
    )
    return jax.shard_map(
        per_device, mesh=mesh, in_specs=placed, out_specs=P(("grp", "row"), "col"), check_vma=False
    )
```

```python
import jax
import jax.numpy as jnp
from jax import lax
from jax.experimental import pallas as pl
from jax.experimental.pallas import tpu as pltpu
from jax.sharding import PartitionSpec as P

MESH = pl.DeviceIdType.MESH
F32 = jnp.float32
BF16 = jnp.bfloat16


def kernel(acts, grads, actb, gradb, out, *scratch):
    (gsrc, xs, gq, bas, gp, gs, gr, gt, av, actv, ap, ar, abs_, abr, aown, axs, agat,
     ob, obr, oacc, zsnd, fin,
     ld, xs_s, xs_r, za_s, za_r, xg_s, xg_r, bz_s, bz_r, bb_s, bb_r, kb_s, kb_r, ak_s, ak_r, ab_s, ab_r,
     ax_s, ax_r, az_s, az_r, axg_s, axg_r, h_s, h_r, gt_s, gt_r, ob_s, ob_r, oz_s, oz_r) = scratch
    x = lax.axis_index("grp")
    r = lax.axis_index("row")
    c = lax.axis_index("col")
    b, k, h, z = r // 2, r % 2, c // 8, c % 8
    p = (b + h) % 2
    scale = 1.0 / 16384.0

    def dev(x_, b_, k_, h_, z_):
        return (x_, 2 * b_ + k_, 8 * h_ + z_)

    core_peer = dev(x, b, 1 - k, h, z)
    b_peer = dev(x, 1 - b, k, h, z)
    h_peer = dev(x, 1 - b, k, 1 - h, z)
    xp, xm, x2 = (x + 1) % 4, (x + 3) % 4, (x + 2) % 4
    xp_peer, xm_peer = dev(xp, b, k, h, z), dev(xm, b, k, h, z)
    zp_peer, zm_peer = dev(x, b, k, h, (z + 1) % 8), dev(x, b, k, h, (z + 7) % 8)

    def cp(src, dst, ss, rs, to):
        return pltpu.make_async_remote_copy(
            src_ref=src, dst_ref=dst, send_sem=ss, recv_sem=rs, device_id=to, device_id_type=MESH)

    sent = []

    def send(src, dst, ss, rs, to):
        d = cp(src, dst, ss, rs, to)
        d.start()
        sent.append(d)

    def got(dst, rs):
        cp(dst, dst, ld.at[9], rs, core_peer).wait_recv()

    l_g = pltpu.make_async_copy(grads.at[pl.ds(2 * p, 2), :, k], gsrc, ld.at[0])
    l_x = pltpu.make_async_copy(grads.at[pl.ds(2 * p, 2), x, k], xs.at[x], ld.at[1])
    rb_own = 2 * b + k
    l_b = pltpu.make_async_copy(gradb, bas.at[rb_own, pl.ds(pl.multiple_of(z * 256, 256), 256), :], ld.at[2])
    l_ab = pltpu.make_async_copy(actb, actv, ld.at[3])
    order = (2 * (1 - p) + 1 - k, 2 * (1 - p) + k, 2 * p + 1 - k, 2 * p + k)
    l_a = [pltpu.make_async_copy(acts.at[s], av.at[i], ld.at[4 + i]) for i, s in enumerate(order)]
    for d in [l_g, l_x, l_b, l_ab] + l_a:
        d.start()

    bar = pltpu.get_barrier_semaphore()

    def sig(to):
        pl.semaphore_signal(bar, inc=1, device_id=to, device_id_type=MESH)

    for to in (core_peer, b_peer, h_peer, xp_peer, xm_peer, dev(x2, b, k, h, z)):
        sig(to)

    @pl.loop(1, 8)
    def _(d):
        zt = (z + d) % 8
        sig(dev(x, b, k, h, zt))
        sig(dev(x, b, 1 - k, h, zt))

    pl.semaphore_wait(bar, 20)

    l_g.wait()
    for dx in (1, 3, 2):
        xt = (x + dx) % 4
        send(gsrc.at[:, xt], xs.at[x], xs_s.at[dx], xs_r.at[dx], dev(xt, b, k, h, z))

    def unit(rb, zs):
        return bas.at[rb, pl.ds(pl.multiple_of(zs * 256, 256), 256), :]

    def half(rb, zs, i):
        return bas.at[rb, pl.ds(pl.multiple_of(zs * 256 + 128 * i, 128), 128), :]

    rb_other = 2 * (1 - b) + k

    def b_send(zs):
        send(unit(rb_own, zs), unit(rb_own, zs), bb_s.at[zs], bb_r.at[zs], b_peer)

    def ring(d):
        fwd, bwd = (z - d + 8) % 8, (z + d) % 8
        if d == 0:
            l_b.wait()
            send(unit(rb_own, z), unit(rb_own, z), bz_s.at[0, 0], bz_r.at[0, 0], zp_peer)
            send(unit(rb_own, z), unit(rb_own, z), bz_s.at[1, 0], bz_r.at[1, 0], zm_peer)
        elif d < 3:
            got(unit(rb_own, fwd), bz_r.at[0, d - 1])
            send(unit(rb_own, fwd), unit(rb_own, fwd), bz_s.at[0, d], bz_r.at[0, d], zp_peer)
            got(unit(rb_own, bwd), bz_r.at[1, d - 1])
            send(unit(rb_own, bwd), unit(rb_own, bwd), bz_s.at[1, d], bz_r.at[1, d], zm_peer)
            b_send(fwd)
            b_send(bwd)
        elif d == 3:
            got(unit(rb_own, fwd), bz_r.at[0, 2])
            send(half(rb_own, fwd, 0), half(rb_own, fwd, 0), bz_s.at[0, 3], bz_r.at[0, 3], zp_peer)
            got(unit(rb_own, bwd), bz_r.at[1, 2])
            send(half(rb_own, bwd, 1), half(rb_own, bwd, 1), bz_s.at[1, 3], bz_r.at[1, 3], zm_peer)
            b_send(fwd)
            b_send(bwd)
        else:
            got(half(rb_own, fwd, 0), bz_r.at[0, 3])
            got(half(rb_own, fwd, 1), bz_r.at[1, 3])
            b_send(fwd)
            send(bas.at[rb_own], bas.at[rb_own], kb_s.at[0], kb_r.at[0], core_peer)

    lane = pl.ds(pl.multiple_of(z * 256, 256), 256)

    def za_copy(e, j):
        zt = 2 * e + j
        return cp(xs.at[e, j], gq.at[x, :, lane], za_s.at[zt], za_r.at[(zt + 8 - z) % 8], dev(x, b, k, h, zt))

    def za(e):
        for j in range(2):
            @pl.when(2 * e + j != z)
            def _():
                za_copy(e, j).start()

            @pl.when(2 * e + j == z)
            def _():
                gq[x, :, lane] = xs[e, j]

    pieces = (0, 1, 7, 2, 6, 3, 5, 4)

    def gpiece(q, d):
        zs = (z + 8 - d) % 8
        return gq.at[q, :, pl.ds(pl.multiple_of(zs * 256, 256), 256)]

    def xg(i):
        d = pieces[i]
        if d:
            got(gpiece(x, d), za_r.at[d])
        send(gpiece(x, d), gpiece(x, d), xg_s.at[0, d], xg_r.at[0, d], xp_peer)
        send(gpiece(x, d), gpiece(x, d), xg_s.at[1, d], xg_r.at[1, d], xm_peer)

    def xg_forward(i):
        d = pieces[i]
        if i % 2 == 0:
            got(gpiece(xm, d), xg_r.at[0, d])
            send(gpiece(xm, d), gpiece(xm, d), xg_s.at[2, d], xg_r.at[2, d], xp_peer)
        else:
            got(gpiece(xp, d), xg_r.at[1, d])
            send(gpiece(xp, d), gpiece(xp, d), xg_s.at[2, d], xg_r.at[2, d], xm_peer)

    def xg_rest(side):
        for i, d in enumerate(pieces):
            if side == 2 or i % 2 != side:
                got(gpiece((xm, xp, x2)[side], d), xg_r.at[side, d])

    def a_part(i):
        if i == 0:
            l_ab.wait()
        l_a[i].wait()

        @pl.loop(0, 4)
        def _(m):
            rows = pl.ds(pl.multiple_of(m * 256, 256), 256)
            ap[i, rows, :] = jnp.dot(av[i, rows, :], actv[...], preferred_element_type=F32)

        if i % 2 == 0:
            send(ap.at[i], ar.at[i // 2], ak_s.at[i // 2], ak_r.at[i // 2], core_peer)

    def a_to_b():
        got(ar.at[0], ak_r.at[0])

        @pl.loop(0, 4)
        def _(m):
            rows = pl.ds(pl.multiple_of(m * 256, 256), 256)
            abs_[rows, :] = (ap[1, rows, :] + ar[0, rows, :]).astype(BF16)

        send(abs_, abr, ab_s, ab_r, b_peer)

    def a_sum():
        got(ar.at[1], ak_r.at[1])
        got(abr, ab_r)

        @pl.loop(0, 4)
        def _(m):
            rows = pl.ds(pl.multiple_of(m * 256, 256), 256)
            aown[m] = (ap[3, rows, :] + ar[1, rows, :] + abr[rows, :].astype(F32)).astype(BF16)

        for dx in (1, 3, 2):
            xt = (x + dx) % 4
            send(aown.at[xt], axs.at[x], ax_s.at[dx], ax_r.at[dx], dev(xt, b, k, h, z))
        axs[x] = aown[x]

    quarter = pl.ds(pl.multiple_of(x * 256, 256), 256)

    def az_copy(e):
        return cp(axs.at[e], agat.at[z // 2, quarter, :], az_s.at[e], az_r.at[z // 2], dev(x, b, z % 2, h, 2 * e + k))

    def az(e):
        @pl.when(2 * e + k != z)
        def _():
            az_copy(e).start()

        @pl.when(2 * e + k == z)
        def _():
            agat[z // 2, quarter, :] = axs[e]

    def apiece(q, u):
        return agat.at[u, pl.ds(pl.multiple_of(q * 256, 256), 256), :]

    def axg(u):
        @pl.when(2 * u + k != z)
        def _():
            got(agat.at[u, quarter, :], az_r.at[u])

        send(apiece(x, u), apiece(x, u), axg_s.at[0, u], axg_r.at[0, u], xp_peer)
        send(apiece(x, u), apiece(x, u), axg_s.at[1, u], axg_r.at[1, u], xm_peer)

    def axg_forward(u):
        if u % 2 == 0:
            got(apiece(xm, u), axg_r.at[0, u])
            send(apiece(xm, u), apiece(xm, u), axg_s.at[2, u], axg_r.at[2, u], xp_peer)
        else:
            got(apiece(xp, u), axg_r.at[1, u])
            send(apiece(xp, u), apiece(xp, u), axg_s.at[2, u], axg_r.at[2, u], xm_peer)

    def axg_rest(u):
        if u % 2 == 0:
            got(apiece(xp, u), axg_r.at[1, u])
        else:
            got(apiece(xm, u), axg_r.at[0, u])
        got(apiece(x2, u), axg_r.at[2, u])

    quarters = (x, xm, xp, x2)

    def g_part(qi, i):
        q, bb = quarters[qi], (b, 1 - b)[i]
        for kk in range(2):
            rb = 2 * bb + kk
            part = jnp.dot(gq[q], bas[rb], preferred_element_type=F32)
            gp[q, rb] = part
            gs[q, rb] = part.astype(BF16)
        pair = pl.ds(2 * bb, 2)
        send(gs.at[q, pair], gr.at[q, pair], h_s.at[qi, i], h_r.at[qi, i], h_peer)

    def tok(q, kk):
        return pl.ds(pl.multiple_of(q * 256 + kk * 128, 128), 128)

    def g_done(qi, i):
        q, bb = quarters[qi], (1 - b, b)[i]
        pair = pl.ds(2 * bb, 2)
        got(gr.at[q, pair], h_r.at[qi, i])
        for kk in range(2):
            rb = 2 * bb + kk
            g = (gp[q, rb] + gr[q, rb].astype(F32)).astype(BF16)
            gt[rb, :, tok(q, k)] = g.T
        mine = gt.at[pair, :, tok(q, k)]
        send(mine, mine, gt_s.at[qi, i], gt_r.at[qi, i], core_peer)

    def g_shared(i):
        pair = pl.ds(2 * (1 - b, b)[i], 2)
        for qi in range(4):
            got(gt.at[pair, :, tok(quarters[qi], 1 - k)], gt_r.at[qi, i])

    def tile(rb, u):
        t = jnp.dot(gt[rb], agat[u], preferred_element_type=F32)
        return t * t * scale

    def ob_send(u):
        for kk in range(2):
            ob[u, kk] = tile(2 * (1 - b) + kk, u).astype(BF16)
        send(ob.at[u], obr.at[u], ob_s.at[u], ob_r.at[u], b_peer)

    def oz_copy(u, kk):
        return cp(zsnd.at[u, kk], fin.at[z], oz_s.at[u, kk], oz_r.at[z], dev(x, b, kk, h, 2 * u + k))

    def here(u, kk):
        return jnp.logical_and(2 * u + k == z, kk == k)

    def oz(u):
        for kk in range(2):
            oacc[kk] = tile(2 * b + kk, u)
        got(obr.at[u], ob_r.at[u])
        for kk in range(2):
            zsnd[u, kk] = (oacc[kk] + obr[u, kk].astype(F32)).astype(BF16)

            @pl.when(jnp.logical_not(here(u, kk)))
            def _():
                oz_copy(u, kk).start()

            @pl.when(here(u, kk))
            def _():
                fin[z] = zsnd[u, kk]

    ring(0)
    l_x.wait()
    za(x)
    a_part(0)
    a_part(1)
    a_to_b()
    got(xs.at[xm], xs_r.at[1])
    za(xm)
    got(xs.at[xp], xs_r.at[3])
    za(xp)
    ring(1)
    got(xs.at[x2], xs_r.at[2])
    za(x2)
    b_send(z)
    xg(0)
    xg(1)
    ring(2)
    xg(2)
    a_part(2)
    xg_forward(0)
    xg(3)
    xg_forward(1)
    a_part(3)
    ring(3)
    xg(4)
    xg_forward(2)
    a_sum()
    xg(5)
    xg_forward(3)
    ring(4)
    xg(6)
    xg_forward(4)
    xg(7)
    xg_forward(5)
    az(x)
    got(axs.at[xm], ax_r.at[1])
    az(xm)
    got(axs.at[xp], ax_r.at[3])
    az(xp)
    xg_forward(6)
    got(axs.at[x2], ax_r.at[2])
    az(x2)
    xg_forward(7)
    got(bas.at[2 * b + 1 - k], kb_r.at[0])
    g_part(0, 0)
    xg_rest(0)
    g_part(1, 0)
    xg_rest(1)
    g_part(2, 0)
    xg_rest(2)
    g_part(3, 0)
    axg(0)
    axg(1)
    axg_forward(0)

    @pl.loop(0, 8)
    def _(zs):
        got(unit(rb_other, zs), bb_r.at[zs])

    send(bas.at[rb_other], bas.at[rb_other], kb_s.at[1], kb_r.at[1], core_peer)
    axg(2)
    axg_forward(1)
    got(bas.at[2 * (1 - b) + 1 - k], kb_r.at[1])
    for qi in range(4):
        g_part(qi, 1)
    axg(3)
    axg_forward(2)
    for qi in range(4):
        g_done(qi, 0)
    axg_forward(3)
    g_shared(0)
    axg_rest(0)
    ob_send(0)
    axg_rest(1)
    ob_send(1)
    for qi in range(4):
        g_done(qi, 1)
    axg_rest(2)
    ob_send(2)
    axg_rest(3)
    ob_send(3)
    g_shared(1)
    for u in range(4):
        oz(u)

    @pl.loop(0, 8)
    def _(zs):
        @pl.when(jnp.logical_not(jnp.logical_and(zs == z, z % 2 == k)))
        def _():
            got(fin.at[zs], oz_r.at[zs])

    total = fin[0].astype(F32)
    for i in range(1, 8):
        total = total + fin[i].astype(F32)
    out[...] = total

    for d in sent:
        d.wait_send()

    for e in range(4):
        for j in range(2):
            @pl.when(2 * e + j != z)
            def _():
                za_copy(e, j).wait_send()

        @pl.when(2 * e + k != z)
        def _():
            az_copy(e).wait_send()

    for u in range(4):
        for kk in range(2):
            @pl.when(jnp.logical_not(here(u, kk)))
            def _():
                oz_copy(u, kk).wait_send()


def per_device(acts, grads, act_basis, grad_basis):
    grads = grads.reshape(4, 4, 2, 128, 256)
    V = pltpu.VMEM
    DMA = pltpu.SemaphoreType.DMA
    buffers = [
        V((2, 4, 128, 256), BF16), V((4, 2, 128, 256), BF16), V((4, 128, 2048), BF16), V((4, 2048, 256), BF16),
        V((4, 4, 128, 256), F32), V((4, 4, 128, 256), BF16), V((4, 4, 128, 256), BF16), V((4, 256, 1024), BF16),
        V((4, 1024, 1024), BF16), V((1024, 256), BF16), V((4, 1024, 256), F32), V((2, 1024, 256), F32),
        V((1024, 256), BF16), V((1024, 256), BF16), V((4, 256, 256), BF16), V((4, 256, 256), BF16),
        V((4, 1024, 256), BF16),
        V((4, 2, 256, 256), BF16), V((4, 2, 256, 256), BF16), V((2, 256, 256), F32), V((4, 2, 256, 256), BF16),
        V((8, 256, 256), BF16),
    ]
    sems = [DMA((10,)), DMA((4,)), DMA((4,)), DMA((8,)), DMA((8,)), DMA((3, 8)), DMA((3, 8)), DMA((2, 4)), DMA((2, 4)),
            DMA((8,)), DMA((8,)), DMA((2,)), DMA((2,)), DMA((2,)), DMA((2,)), DMA, DMA,
            DMA((4,)), DMA((4,)), DMA((4,)), DMA((4,)), DMA((3, 4)), DMA((3, 4)), DMA((4, 2)), DMA((4, 2)),
            DMA((4, 2)), DMA((4, 2)), DMA((4,)), DMA((4,)), DMA((4, 2)), DMA((8,))]
    hbm = pl.BlockSpec(memory_space=pl.ANY)
    return pl.pallas_call(
        kernel,
        out_shape=jax.ShapeDtypeStruct((256, 256), F32),
        in_specs=[hbm] * 4,
        out_specs=pl.BlockSpec(memory_space=pltpu.VMEM),
        scratch_shapes=buffers + sems,
        compiler_params=pltpu.CompilerParams(
            collective_id=0, has_side_effects=True, vmem_limit_bytes=56 * 2**20),
        cost_estimate=pl.CostEstimate(flops=6442450944, bytes_accessed=11534336, transcendentals=0),
    )(acts, grads, act_basis, grad_basis)


def solution(mesh):
    placed = (
        P("grp", None, "row"),
        P("grp", None, "col"),
        P("row", "col"),
        P("col", ("grp", "row")),
    )
    return jax.shard_map(
        per_device, mesh=mesh, in_specs=placed, out_specs=P(("grp", "row"), "col"), check_vma=False
    )
```

```python
import jax
import jax.numpy as jnp
from jax import lax
from jax.experimental import pallas as pl
from jax.experimental.pallas import tpu as pltpu
from jax.sharding import PartitionSpec as P

MESH = pl.DeviceIdType.MESH
F32 = jnp.float32
BF16 = jnp.bfloat16


def kernel(acts, grads, actb, gradb, out, *scratch):
    (gsrc, xs, gq, bas, gp, gs, gr, gt, av, actv, ap, ar, abs_, abr, aown, axs, agat,
     ob, obr, oacc, zsnd, fin, mrg,
     ld, xs_s, xs_r, za_s, za_r, xg_s, xg_r, bz_s, bz_r, bb_s, bb_r, kb_s, kb_r, ak_s, ak_r, ab_s, ab_r,
     ax_s, ax_r, az_s, az_r, axg_s, axg_r, h_s, h_r, gt_s, gt_r, ob_s, ob_r, oz_s, oz_r, mg_r) = scratch
    x = lax.axis_index("grp")
    r = lax.axis_index("row")
    c = lax.axis_index("col")
    b, k, h, z = r // 2, r % 2, c // 8, c % 8
    p = (b + h) % 2
    scale = 1.0 / 16384.0

    def dev(x_, b_, k_, h_, z_):
        return (x_, 2 * b_ + k_, 8 * h_ + z_)

    core_peer = dev(x, b, 1 - k, h, z)
    b_peer = dev(x, 1 - b, k, h, z)
    h_peer = dev(x, 1 - b, k, 1 - h, z)
    xp, xm, x2 = (x + 1) % 4, (x + 3) % 4, (x + 2) % 4
    xp_peer, xm_peer = dev(xp, b, k, h, z), dev(xm, b, k, h, z)
    zp_peer, zm_peer = dev(x, b, k, h, (z + 1) % 8), dev(x, b, k, h, (z + 7) % 8)

    def cp(src, dst, ss, rs, to):
        return pltpu.make_async_remote_copy(
            src_ref=src, dst_ref=dst, send_sem=ss, recv_sem=rs, device_id=to, device_id_type=MESH)

    sent = []

    def send(src, dst, ss, rs, to):
        d = cp(src, dst, ss, rs, to)
        d.start()
        sent.append(d)

    def got(dst, rs):
        cp(dst, dst, ld.at[9], rs, core_peer).wait_recv()

    l_g = pltpu.make_async_copy(grads.at[pl.ds(2 * p, 2), :, k], gsrc, ld.at[0])
    l_x = pltpu.make_async_copy(grads.at[pl.ds(2 * p, 2), x, k], xs.at[x], ld.at[1])
    rb_own = 2 * b + k
    l_b = pltpu.make_async_copy(gradb, bas.at[rb_own, pl.ds(pl.multiple_of(z * 256, 256), 256), :], ld.at[2])
    l_ab = pltpu.make_async_copy(actb, actv, ld.at[3])
    order = (2 * (1 - p) + 1 - k, 2 * (1 - p) + k, 2 * p + 1 - k, 2 * p + k)
    l_a = [pltpu.make_async_copy(acts.at[s], av.at[i], ld.at[4 + i]) for i, s in enumerate(order)]
    for d in [l_g, l_x, l_b, l_ab] + l_a:
        d.start()

    bar = pltpu.get_barrier_semaphore()

    def sig(to):
        pl.semaphore_signal(bar, inc=1, device_id=to, device_id_type=MESH)

    for to in (core_peer, b_peer, h_peer, xp_peer, xm_peer, dev(x2, b, k, h, z)):
        sig(to)

    @pl.loop(1, 8)
    def _(d):
        zt = (z + d) % 8
        sig(dev(x, b, k, h, zt))
        sig(dev(x, b, 1 - k, h, zt))

    pl.semaphore_wait(bar, 20)

    l_g.wait()
    for dx in (1, 3, 2):
        xt = (x + dx) % 4
        send(gsrc.at[:, xt], xs.at[x], xs_s.at[dx], xs_r.at[dx], dev(xt, b, k, h, z))

    def unit(rb, zs):
        return bas.at[rb, pl.ds(pl.multiple_of(zs * 256, 256), 256), :]

    def half(rb, zs, i):
        return bas.at[rb, pl.ds(pl.multiple_of(zs * 256 + 128 * i, 128), 128), :]

    rb_other = 2 * (1 - b) + k

    def b_send(zs):
        send(unit(rb_own, zs), unit(rb_own, zs), bb_s.at[zs], bb_r.at[zs], b_peer)

    def ring(d):
        fwd, bwd = (z - d + 8) % 8, (z + d) % 8
        if d == 0:
            l_b.wait()
            send(unit(rb_own, z), unit(rb_own, z), bz_s.at[0, 0], bz_r.at[0, 0], zp_peer)
            send(unit(rb_own, z), unit(rb_own, z), bz_s.at[1, 0], bz_r.at[1, 0], zm_peer)
        elif d < 3:
            got(unit(rb_own, fwd), bz_r.at[0, d - 1])
            send(unit(rb_own, fwd), unit(rb_own, fwd), bz_s.at[0, d], bz_r.at[0, d], zp_peer)
            got(unit(rb_own, bwd), bz_r.at[1, d - 1])
            send(unit(rb_own, bwd), unit(rb_own, bwd), bz_s.at[1, d], bz_r.at[1, d], zm_peer)
            b_send(fwd)
            b_send(bwd)
        elif d == 3:
            got(unit(rb_own, fwd), bz_r.at[0, 2])
            send(half(rb_own, fwd, 0), half(rb_own, fwd, 0), bz_s.at[0, 3], bz_r.at[0, 3], zp_peer)
            got(unit(rb_own, bwd), bz_r.at[1, 2])
            send(half(rb_own, bwd, 1), half(rb_own, bwd, 1), bz_s.at[1, 3], bz_r.at[1, 3], zm_peer)
            b_send(fwd)
            b_send(bwd)
        else:
            got(half(rb_own, fwd, 0), bz_r.at[0, 3])
            got(half(rb_own, fwd, 1), bz_r.at[1, 3])
            b_send(fwd)
            send(bas.at[rb_own], bas.at[rb_own], kb_s.at[0], kb_r.at[0], core_peer)

    lane = pl.ds(pl.multiple_of(z * 256, 256), 256)

    def za_copy(e, j):
        zt = 2 * e + j
        return cp(xs.at[e, j], gq.at[x, :, lane], za_s.at[zt], za_r.at[(zt + 8 - z) % 8], dev(x, b, k, h, zt))

    def za(e):
        for j in range(2):
            @pl.when(2 * e + j != z)
            def _():
                za_copy(e, j).start()

            @pl.when(2 * e + j == z)
            def _():
                gq[x, :, lane] = xs[e, j]

    pieces = (0, 1, 7, 2, 6, 3, 5, 4)

    def gpiece(q, d):
        zs = (z + 8 - d) % 8
        return gq.at[q, :, pl.ds(pl.multiple_of(zs * 256, 256), 256)]

    def xg(i):
        d = pieces[i]
        if d:
            got(gpiece(x, d), za_r.at[d])
        send(gpiece(x, d), gpiece(x, d), xg_s.at[0, d], xg_r.at[0, d], xp_peer)
        send(gpiece(x, d), gpiece(x, d), xg_s.at[1, d], xg_r.at[1, d], xm_peer)

    def xg_forward(i):
        d = pieces[i]
        if i % 2 == 0:
            got(gpiece(xm, d), xg_r.at[0, d])
            send(gpiece(xm, d), gpiece(xm, d), xg_s.at[2, d], xg_r.at[2, d], xp_peer)
        else:
            got(gpiece(xp, d), xg_r.at[1, d])
            send(gpiece(xp, d), gpiece(xp, d), xg_s.at[2, d], xg_r.at[2, d], xm_peer)

    def xg_rest(side):
        for i, d in enumerate(pieces):
            if side == 2 or i % 2 != side:
                got(gpiece((xm, xp, x2)[side], d), xg_r.at[side, d])

    def a_part(i):
        if i == 0:
            l_ab.wait()
        l_a[i].wait()

        @pl.loop(0, 4)
        def _(m):
            rows = pl.ds(pl.multiple_of(m * 256, 256), 256)
            ap[i, rows, :] = jnp.dot(av[i, rows, :], actv[...], preferred_element_type=F32)

        if i % 2 == 0:
            send(ap.at[i], ar.at[i // 2], ak_s.at[i // 2], ak_r.at[i // 2], core_peer)

    def a_to_b():
        got(ar.at[0], ak_r.at[0])

        @pl.loop(0, 4)
        def _(m):
            rows = pl.ds(pl.multiple_of(m * 256, 256), 256)
            abs_[rows, :] = (ap[1, rows, :] + ar[0, rows, :]).astype(BF16)

        send(abs_, abr, ab_s, ab_r, b_peer)

    def a_sum():
        got(ar.at[1], ak_r.at[1])
        got(abr, ab_r)

        @pl.loop(0, 4)
        def _(m):
            rows = pl.ds(pl.multiple_of(m * 256, 256), 256)
            aown[m] = (ap[3, rows, :] + ar[1, rows, :] + abr[rows, :].astype(F32)).astype(BF16)

        for dx in (1, 3, 2):
            xt = (x + dx) % 4
            send(aown.at[xt], axs.at[x], ax_s.at[dx], ax_r.at[dx], dev(xt, b, k, h, z))
        axs[x] = aown[x]

    quarter = pl.ds(pl.multiple_of(x * 256, 256), 256)

    def az_copy(e):
        return cp(axs.at[e], agat.at[z // 2, quarter, :], az_s.at[e], az_r.at[z // 2], dev(x, b, z % 2, h, 2 * e + k))

    def az(e):
        @pl.when(2 * e + k != z)
        def _():
            az_copy(e).start()

        @pl.when(2 * e + k == z)
        def _():
            agat[z // 2, quarter, :] = axs[e]

    even = 1 - (z + k) % 2
    far = (3 + even, 5 - 3 * even, 1 + 5 * even, 7 - 7 * even)
    units = tuple((z + f) % 8 // 2 for f in far)

    def apiece(q, i):
        return agat.at[units[i], pl.ds(pl.multiple_of(q * 256, 256), 256), :]

    def axg(i):
        @pl.when(2 * units[i] + k != z)
        def _():
            got(apiece(x, i), az_r.at[units[i]])

        send(apiece(x, i), apiece(x, i), axg_s.at[0, i], axg_r.at[0, i], xp_peer)
        send(apiece(x, i), apiece(x, i), axg_s.at[1, i], axg_r.at[1, i], xm_peer)

    def axg_forward(i):
        if i % 2 == 0:
            got(apiece(xm, i), axg_r.at[0, i])
            send(apiece(xm, i), apiece(xm, i), axg_s.at[2, i], axg_r.at[2, i], xp_peer)
        else:
            got(apiece(xp, i), axg_r.at[1, i])
            send(apiece(xp, i), apiece(xp, i), axg_s.at[2, i], axg_r.at[2, i], xm_peer)

    def axg_rest(i):
        if i % 2 == 0:
            got(apiece(xp, i), axg_r.at[1, i])
        else:
            got(apiece(xm, i), axg_r.at[0, i])
        got(apiece(x2, i), axg_r.at[2, i])

    quarters = (x, xm, xp, x2)

    def g_part(qi, i):
        q, bb = quarters[qi], (b, 1 - b)[i]
        for kk in range(2):
            rb = 2 * bb + kk
            part = jnp.dot(gq[q], bas[rb], preferred_element_type=F32)
            gp[q, rb] = part
            gs[q, rb] = part.astype(BF16)
        pair = pl.ds(2 * bb, 2)
        send(gs.at[q, pair], gr.at[q, pair], h_s.at[qi, i], h_r.at[qi, i], h_peer)

    def tok(q, kk):
        return pl.ds(pl.multiple_of(q * 256 + kk * 128, 128), 128)

    def g_done(qi, i):
        q, bb = quarters[qi], (1 - b, b)[i]
        pair = pl.ds(2 * bb, 2)
        got(gr.at[q, pair], h_r.at[qi, i])
        for kk in range(2):
            rb = 2 * bb + kk
            g = (gp[q, rb] + gr[q, rb].astype(F32)).astype(BF16)
            gt[rb, :, tok(q, k)] = g.T
        mine = gt.at[pair, :, tok(q, k)]
        send(mine, mine, gt_s.at[qi, i], gt_r.at[qi, i], core_peer)

    def g_shared(i):
        pair = pl.ds(2 * (1 - b, b)[i], 2)
        for qi in range(4):
            got(gt.at[pair, :, tok(quarters[qi], 1 - k)], gt_r.at[qi, i])

    def tile(rb, u):
        t = jnp.dot(gt[rb], agat[u], preferred_element_type=F32)
        return t * t * scale

    def ob_send(i):
        for kk in range(2):
            ob[i, kk] = tile(2 * (1 - b) + kk, units[i]).astype(BF16)
            send(ob.at[i, kk], obr.at[i, kk], ob_s.at[i, kk], ob_r.at[i, kk], b_peer)

    def oz_copy(i, kk):
        return cp(zsnd.at[i, kk], fin.at[z], oz_s.at[i, kk], oz_r.at[z], dev(x, b, kk, h, (z + far[i]) % 8))

    def merge_copy(i, kk):
        return cp(zsnd.at[i, kk], mrg.at[i, kk], oz_s.at[i, kk], mg_r.at[i, kk], (zp_peer, zm_peer)[i])

    def here(i, kk):
        return jnp.logical_and(even == 1, kk == k)

    def oz(i):
        for kk in range(2):
            oacc[...] = tile(2 * b + kk, units[i])
            got(obr.at[i, kk], ob_r.at[i, kk])
            v = oacc[...] + obr[i, kk].astype(F32)
            zsnd[i, kk] = v.astype(BF16)
            if i in (1, 2):
                oacc[...] = v

                @pl.when(even == 1)
                def _():
                    got(mrg.at[i - 1, kk], mg_r.at[i - 1, kk])
                    zsnd[i, kk] = (oacc[...] + mrg[i - 1, kk].astype(F32)).astype(BF16)

            if i < 2:
                @pl.when(even == 0)
                def _():
                    merge_copy(i, kk).start()

                @pl.when(even == 1)
                def _():
                    oz_copy(i, kk).start()
            elif i == 2:
                oz_copy(i, kk).start()
            else:
                @pl.when(jnp.logical_not(here(i, kk)))
                def _():
                    oz_copy(i, kk).start()

                @pl.when(here(i, kk))
                def _():
                    fin[z] = zsnd[i, kk]

    ring(0)
    l_x.wait()
    za(x)
    a_part(0)
    a_part(1)
    a_to_b()
    got(xs.at[xm], xs_r.at[1])
    za(xm)
    got(xs.at[xp], xs_r.at[3])
    za(xp)
    ring(1)
    got(xs.at[x2], xs_r.at[2])
    za(x2)
    b_send(z)
    xg(0)
    xg(1)
    ring(2)
    xg(2)
    a_part(2)
    xg_forward(0)
    xg(3)
    xg_forward(1)
    a_part(3)
    ring(3)
    xg(4)
    xg_forward(2)
    a_sum()
    xg(5)
    xg_forward(3)
    ring(4)
    xg(6)
    xg_forward(4)
    xg(7)
    xg_forward(5)
    az(x)
    got(axs.at[xm], ax_r.at[1])
    az(xm)
    got(axs.at[xp], ax_r.at[3])
    az(xp)
    xg_forward(6)
    got(axs.at[x2], ax_r.at[2])
    az(x2)
    xg_forward(7)
    got(bas.at[2 * b + 1 - k], kb_r.at[0])
    g_part(0, 0)
    xg_rest(0)
    g_part(1, 0)
    xg_rest(1)
    g_part(2, 0)
    xg_rest(2)
    g_part(3, 0)
    axg(0)
    axg(1)
    axg_forward(0)

    @pl.loop(0, 8)
    def _(zs):
        got(unit(rb_other, zs), bb_r.at[zs])

    send(bas.at[rb_other], bas.at[rb_other], kb_s.at[1], kb_r.at[1], core_peer)
    axg(2)
    axg_forward(1)
    got(bas.at[2 * (1 - b) + 1 - k], kb_r.at[1])
    for qi in range(4):
        g_part(qi, 1)
    axg(3)
    for qi in range(4):
        g_done(qi, 0)
    g_shared(0)
    axg_forward(2)
    axg_rest(0)
    ob_send(0)
    axg_forward(3)
    axg_rest(1)
    ob_send(1)
    for qi in range(4):
        g_done(qi, 1)
    axg_rest(2)
    ob_send(2)
    axg_rest(3)
    ob_send(3)
    g_shared(1)
    for u in range(4):
        oz(u)

    total = None
    for off in (4, 2, 6, 1, 7, 0):
        zs = (z + off) % 8
        if off:
            got(fin.at[zs], oz_r.at[zs])
        else:
            @pl.when(even == 0)
            def _():
                got(fin.at[z], oz_r.at[z])
        part = fin[zs].astype(F32)
        total = part if total is None else total + part
    out[...] = total

    for d in sent:
        d.wait_send()

    for e in range(4):
        for j in range(2):
            @pl.when(2 * e + j != z)
            def _():
                za_copy(e, j).wait_send()

        @pl.when(2 * e + k != z)
        def _():
            az_copy(e).wait_send()

    for i in range(4):
        for kk in range(2):
            if i < 3:
                oz_copy(i, kk).wait_send()
            else:
                @pl.when(jnp.logical_not(here(i, kk)))
                def _():
                    oz_copy(i, kk).wait_send()


def per_device(acts, grads, act_basis, grad_basis):
    grads = grads.reshape(4, 4, 2, 128, 256)
    V = pltpu.VMEM
    DMA = pltpu.SemaphoreType.DMA
    buffers = [
        V((2, 4, 128, 256), BF16), V((4, 2, 128, 256), BF16), V((4, 128, 2048), BF16), V((4, 2048, 256), BF16),
        V((4, 4, 128, 256), F32), V((4, 4, 128, 256), BF16), V((4, 4, 128, 256), BF16), V((4, 256, 1024), BF16),
        V((4, 1024, 1024), BF16), V((1024, 256), BF16), V((4, 1024, 256), F32), V((2, 1024, 256), F32),
        V((1024, 256), BF16), V((1024, 256), BF16), V((4, 256, 256), BF16), V((4, 256, 256), BF16),
        V((4, 1024, 256), BF16),
        V((4, 2, 256, 256), BF16), V((4, 2, 256, 256), BF16), V((256, 256), F32), V((4, 2, 256, 256), BF16),
        V((8, 256, 256), BF16), V((2, 2, 256, 256), BF16),
    ]
    sems = [DMA((10,)), DMA((4,)), DMA((4,)), DMA((8,)), DMA((8,)), DMA((3, 8)), DMA((3, 8)), DMA((2, 4)), DMA((2, 4)),
            DMA((8,)), DMA((8,)), DMA((2,)), DMA((2,)), DMA((2,)), DMA((2,)), DMA, DMA,
            DMA((4,)), DMA((4,)), DMA((4,)), DMA((4,)), DMA((3, 4)), DMA((3, 4)), DMA((4, 2)), DMA((4, 2)),
            DMA((4, 2)), DMA((4, 2)), DMA((4, 2)), DMA((4, 2)), DMA((4, 2)), DMA((8,)), DMA((2, 2))]
    hbm = pl.BlockSpec(memory_space=pl.ANY)
    return pl.pallas_call(
        kernel,
        out_shape=jax.ShapeDtypeStruct((256, 256), F32),
        in_specs=[hbm] * 4,
        out_specs=pl.BlockSpec(memory_space=pltpu.VMEM),
        scratch_shapes=buffers + sems,
        compiler_params=pltpu.CompilerParams(
            collective_id=0, has_side_effects=True, vmem_limit_bytes=56 * 2**20),
        cost_estimate=pl.CostEstimate(flops=6442450944, bytes_accessed=11534336, transcendentals=0),
    )(acts, grads, act_basis, grad_basis)


def solution(mesh):
    placed = (
        P("grp", None, "row"),
        P("grp", None, "col"),
        P("row", "col"),
        P("col", ("grp", "row")),
    )
    return jax.shard_map(
        per_device, mesh=mesh, in_specs=placed, out_specs=P(("grp", "row"), "col"), check_vma=False
    )
```

```python
import jax
import jax.numpy as jnp
from jax import lax
from jax.experimental import pallas as pl
from jax.experimental.pallas import tpu as pltpu
from jax.sharding import PartitionSpec as P

MESH = pl.DeviceIdType.MESH
F32 = jnp.float32
BF16 = jnp.bfloat16


def kernel(acts, grads, actb, gradb, out, *scratch):
    (gsrc, xs, gq, bas, gp, gs, gr, gt, av, actv, ap, ar, abs_, abr, aown, axs, agat,
     ob, obr, oacc, zsnd, fin, mrg,
     ld, xs_s, xs_r, za_s, za_r, xg_s, xg_r, bz_s, bz_r, bb_s, bb_r, kb_s, kb_r, ak_s, ak_r, ab_s, ab_r,
     ax_s, ax_r, az_s, az_r, axg_s, axg_r, h_s, h_r, gt_s, gt_r, ob_s, ob_r, oz_s, oz_r, mg_r) = scratch
    x = lax.axis_index("grp")
    r = lax.axis_index("row")
    c = lax.axis_index("col")
    b, k, h, z = r // 2, r % 2, c // 8, c % 8
    p = (b + h) % 2
    scale = 1.0 / 16384.0

    def dev(x_, b_, k_, h_, z_):
        return (x_, 2 * b_ + k_, 8 * h_ + z_)

    core_peer = dev(x, b, 1 - k, h, z)
    b_peer = dev(x, 1 - b, k, h, z)
    h_peer = dev(x, 1 - b, k, 1 - h, z)
    xp, xm, x2 = (x + 1) % 4, (x + 3) % 4, (x + 2) % 4
    xp_peer, xm_peer = dev(xp, b, k, h, z), dev(xm, b, k, h, z)
    zp_peer, zm_peer = dev(x, b, k, h, (z + 1) % 8), dev(x, b, k, h, (z + 7) % 8)

    def cp(src, dst, ss, rs, to):
        return pltpu.make_async_remote_copy(
            src_ref=src, dst_ref=dst, send_sem=ss, recv_sem=rs, device_id=to, device_id_type=MESH)

    sent = []

    def send(src, dst, ss, rs, to):
        d = cp(src, dst, ss, rs, to)
        d.start()
        sent.append(d)

    def got(dst, rs):
        cp(dst, dst, ld.at[9], rs, core_peer).wait_recv()

    l_g = pltpu.make_async_copy(grads.at[pl.ds(2 * p, 2), :, k], gsrc, ld.at[0])
    l_x = pltpu.make_async_copy(grads.at[pl.ds(2 * p, 2), x, k], xs.at[x], ld.at[1])
    rb_own = 2 * b + k
    l_b = pltpu.make_async_copy(gradb, bas.at[rb_own, pl.ds(pl.multiple_of(z * 256, 256), 256), :], ld.at[2])
    l_ab = pltpu.make_async_copy(actb, actv, ld.at[3])
    order = (2 * (1 - p) + 1 - k, 2 * (1 - p) + k, 2 * p + 1 - k, 2 * p + k)
    l_a = [pltpu.make_async_copy(acts.at[s], av.at[i], ld.at[4 + i]) for i, s in enumerate(order)]
    for d in [l_g, l_x, l_b, l_ab] + l_a:
        d.start()

    bar = pltpu.get_barrier_semaphore()

    def sig(to):
        pl.semaphore_signal(bar, inc=1, device_id=to, device_id_type=MESH)

    for to in (core_peer, b_peer, h_peer, xp_peer, xm_peer, dev(x2, b, k, h, z)):
        sig(to)

    @pl.loop(1, 8)
    def _(d):
        zt = (z + d) % 8
        sig(dev(x, b, k, h, zt))
        sig(dev(x, b, 1 - k, h, zt))

    pl.semaphore_wait(bar, 20)

    l_g.wait()
    for dx in (1, 3, 2):
        xt = (x + dx) % 4
        send(gsrc.at[:, xt], xs.at[x], xs_s.at[dx], xs_r.at[dx], dev(xt, b, k, h, z))

    def unit(rb, zs):
        return bas.at[rb, pl.ds(pl.multiple_of(zs * 256, 256), 256), :]

    def half(rb, zs, i):
        return bas.at[rb, pl.ds(pl.multiple_of(zs * 256 + 128 * i, 128), 128), :]

    rb_other = 2 * (1 - b) + k

    def b_send(zs):
        send(unit(rb_own, zs), unit(rb_own, zs), bb_s.at[zs], bb_r.at[zs], b_peer)

    def ring(d):
        fwd, bwd = (z - d + 8) % 8, (z + d) % 8
        if d == 0:
            l_b.wait()
            send(unit(rb_own, z), unit(rb_own, z), bz_s.at[0, 0], bz_r.at[0, 0], zp_peer)
            send(unit(rb_own, z), unit(rb_own, z), bz_s.at[1, 0], bz_r.at[1, 0], zm_peer)
        elif d < 3:
            got(unit(rb_own, fwd), bz_r.at[0, d - 1])
            send(unit(rb_own, fwd), unit(rb_own, fwd), bz_s.at[0, d], bz_r.at[0, d], zp_peer)
            got(unit(rb_own, bwd), bz_r.at[1, d - 1])
            send(unit(rb_own, bwd), unit(rb_own, bwd), bz_s.at[1, d], bz_r.at[1, d], zm_peer)
            b_send(fwd)
            b_send(bwd)
        elif d == 3:
            got(unit(rb_own, fwd), bz_r.at[0, 2])
            send(half(rb_own, fwd, 0), half(rb_own, fwd, 0), bz_s.at[0, 3], bz_r.at[0, 3], zp_peer)
            got(unit(rb_own, bwd), bz_r.at[1, 2])
            send(half(rb_own, bwd, 1), half(rb_own, bwd, 1), bz_s.at[1, 3], bz_r.at[1, 3], zm_peer)
            b_send(fwd)
            b_send(bwd)
        else:
            got(half(rb_own, fwd, 0), bz_r.at[0, 3])
            got(half(rb_own, fwd, 1), bz_r.at[1, 3])
            b_send(fwd)
            send(bas.at[rb_own], bas.at[rb_own], kb_s.at[0], kb_r.at[0], core_peer)

    lane = pl.ds(pl.multiple_of(z * 256, 256), 256)

    def za_copy(e, j):
        zt = 2 * e + j
        return cp(xs.at[e, j], gq.at[x, :, lane], za_s.at[zt], za_r.at[(zt + 8 - z) % 8], dev(x, b, k, h, zt))

    def za(e):
        for j in range(2):
            @pl.when(2 * e + j != z)
            def _():
                za_copy(e, j).start()

            @pl.when(2 * e + j == z)
            def _():
                gq[x, :, lane] = xs[e, j]

    pieces = (0, 1, 7, 2, 6, 3, 5, 4)

    def gpiece(q, d):
        zs = (z + 8 - d) % 8
        return gq.at[q, :, pl.ds(pl.multiple_of(zs * 256, 256), 256)]

    def xg(i):
        d = pieces[i]
        if d:
            got(gpiece(x, d), za_r.at[d])
        send(gpiece(x, d), gpiece(x, d), xg_s.at[0, d], xg_r.at[0, d], xp_peer)
        send(gpiece(x, d), gpiece(x, d), xg_s.at[1, d], xg_r.at[1, d], xm_peer)

    def xg_forward(i):
        d = pieces[i]
        if i % 2 == 0:
            got(gpiece(xm, d), xg_r.at[0, d])
            send(gpiece(xm, d), gpiece(xm, d), xg_s.at[2, d], xg_r.at[2, d], xp_peer)
        else:
            got(gpiece(xp, d), xg_r.at[1, d])
            send(gpiece(xp, d), gpiece(xp, d), xg_s.at[2, d], xg_r.at[2, d], xm_peer)

    def xg_rest(side):
        for i, d in enumerate(pieces):
            if side == 2 or i % 2 != side:
                got(gpiece((xm, xp, x2)[side], d), xg_r.at[side, d])

    def a_part(i):
        if i == 0:
            l_ab.wait()
        l_a[i].wait()

        @pl.loop(0, 4)
        def _(m):
            rows = pl.ds(pl.multiple_of(m * 256, 256), 256)
            ap[i, rows, :] = jnp.dot(av[i, rows, :], actv[...], preferred_element_type=F32)

        if i % 2 == 0:
            send(ap.at[i], ar.at[i // 2], ak_s.at[i // 2], ak_r.at[i // 2], core_peer)

    def a_to_b():
        got(ar.at[0], ak_r.at[0])

        @pl.loop(0, 4)
        def _(m):
            rows = pl.ds(pl.multiple_of(m * 256, 256), 256)
            abs_[rows, :] = (ap[1, rows, :] + ar[0, rows, :]).astype(BF16)

        send(abs_, abr, ab_s, ab_r, b_peer)

    def a_sum():
        got(ar.at[1], ak_r.at[1])
        got(abr, ab_r)

        @pl.loop(0, 4)
        def _(m):
            rows = pl.ds(pl.multiple_of(m * 256, 256), 256)
            aown[m] = (ap[3, rows, :] + ar[1, rows, :] + abr[rows, :].astype(F32)).astype(BF16)

        for dx in (1, 3, 2):
            xt = (x + dx) % 4
            send(aown.at[xt], axs.at[x], ax_s.at[dx], ax_r.at[dx], dev(xt, b, k, h, z))
        axs[x] = aown[x]

    quarter = pl.ds(pl.multiple_of(x * 256, 256), 256)

    def az_copy(e):
        return cp(axs.at[e], agat.at[z // 2, quarter, :], az_s.at[e], az_r.at[z // 2], dev(x, b, z % 2, h, 2 * e + k))

    def az(e):
        @pl.when(2 * e + k != z)
        def _():
            az_copy(e).start()

        @pl.when(2 * e + k == z)
        def _():
            agat[z // 2, quarter, :] = axs[e]

    even = 1 - (z + k) % 2
    far = (3 + even, 5 - 3 * even, 1 + 5 * even, 7 - 7 * even)
    units = tuple((z + f) % 8 // 2 for f in far)

    def apiece(q, i):
        return agat.at[units[i], pl.ds(pl.multiple_of(q * 256, 256), 256), :]

    def axg(i):
        @pl.when(2 * units[i] + k != z)
        def _():
            got(apiece(x, i), az_r.at[units[i]])

        send(apiece(x, i), apiece(x, i), axg_s.at[0, i], axg_r.at[0, i], xp_peer)
        send(apiece(x, i), apiece(x, i), axg_s.at[1, i], axg_r.at[1, i], xm_peer)

    def axg_forward(i):
        if i % 2 == 0:
            got(apiece(xm, i), axg_r.at[0, i])
            send(apiece(xm, i), apiece(xm, i), axg_s.at[2, i], axg_r.at[2, i], xp_peer)
        else:
            got(apiece(xp, i), axg_r.at[1, i])
            send(apiece(xp, i), apiece(xp, i), axg_s.at[2, i], axg_r.at[2, i], xm_peer)

    def axg_rest(i):
        if i % 2 == 0:
            got(apiece(xp, i), axg_r.at[1, i])
        else:
            got(apiece(xm, i), axg_r.at[0, i])
        got(apiece(x2, i), axg_r.at[2, i])

    quarters = (x, xm, xp, x2)

    def g_part(qi, i):
        q, bb = quarters[qi], (b, 1 - b)[i]
        for kk in range(2):
            rb = 2 * bb + kk
            part = jnp.dot(gq[q], bas[rb], preferred_element_type=F32)
            gp[q, rb] = part
            gs[q, rb] = part.astype(BF16)
        pair = pl.ds(2 * bb, 2)
        send(gs.at[q, pair], gr.at[q, pair], h_s.at[qi, i], h_r.at[qi, i], h_peer)

    def tok(q, kk):
        return pl.ds(pl.multiple_of(q * 256 + kk * 128, 128), 128)

    def g_done(qi, i):
        q, bb = quarters[qi], (1 - b, b)[i]
        pair = pl.ds(2 * bb, 2)
        got(gr.at[q, pair], h_r.at[qi, i])
        for kk in range(2):
            rb = 2 * bb + kk
            g = (gp[q, rb] + gr[q, rb].astype(F32)).astype(BF16)
            gt[rb, :, tok(q, k)] = g.T
        mine = gt.at[pair, :, tok(q, k)]
        send(mine, mine, gt_s.at[qi, i], gt_r.at[qi, i], core_peer)

    def g_shared(i):
        pair = pl.ds(2 * (1 - b, b)[i], 2)
        for qi in range(4):
            got(gt.at[pair, :, tok(quarters[qi], 1 - k)], gt_r.at[qi, i])

    def tile(rb, u):
        t = jnp.dot(gt[rb], agat[u], preferred_element_type=F32)
        return t * t * scale

    def ob_send(i):
        for kk in range(2):
            ob[i, kk] = tile(2 * (1 - b) + kk, units[i]).astype(BF16)
            send(ob.at[i, kk], obr.at[i, kk], ob_s.at[i, kk], ob_r.at[i, kk], b_peer)

    def oz_copy(i, kk):
        return cp(zsnd.at[i, kk], fin.at[z], oz_s.at[i, kk], oz_r.at[z], dev(x, b, kk, h, (z + far[i]) % 8))

    def merge_copy(i, kk):
        return cp(zsnd.at[i, kk], mrg.at[i, kk], oz_s.at[i, kk], mg_r.at[i, kk], (zp_peer, zm_peer)[i])

    def here(i, kk):
        return jnp.logical_and(even == 1, kk == k)

    def oz(i):
        for kk in range(2):
            oacc[...] = tile(2 * b + kk, units[i])
            got(obr.at[i, kk], ob_r.at[i, kk])
            v = oacc[...] + obr[i, kk].astype(F32)
            zsnd[i, kk] = v.astype(BF16)
            if i in (1, 2):
                oacc[...] = v

                @pl.when(even == 1)
                def _():
                    got(mrg.at[i - 1, kk], mg_r.at[i - 1, kk])
                    zsnd[i, kk] = (oacc[...] + mrg[i - 1, kk].astype(F32)).astype(BF16)

            if i < 2:
                @pl.when(even == 0)
                def _():
                    merge_copy(i, kk).start()

                @pl.when(even == 1)
                def _():
                    oz_copy(i, kk).start()
            elif i == 2:
                oz_copy(i, kk).start()
            else:
                @pl.when(jnp.logical_not(here(i, kk)))
                def _():
                    oz_copy(i, kk).start()

                @pl.when(here(i, kk))
                def _():
                    fin[z] = zsnd[i, kk]

    ring(0)
    l_x.wait()
    za(x)
    a_part(0)
    a_part(1)
    ring(1)
    a_to_b()
    got(xs.at[xm], xs_r.at[1])
    za(xm)
    got(xs.at[xp], xs_r.at[3])
    za(xp)
    got(xs.at[x2], xs_r.at[2])
    za(x2)
    b_send(z)
    xg(0)
    xg(1)
    ring(2)
    xg(2)
    a_part(2)
    xg_forward(0)
    xg(3)
    xg_forward(1)
    a_part(3)
    ring(3)
    xg(4)
    xg_forward(2)
    a_sum()
    xg(5)
    xg_forward(3)
    ring(4)
    xg(6)
    xg_forward(4)
    xg(7)
    xg_forward(5)
    az(x)
    got(axs.at[xm], ax_r.at[1])
    az(xm)
    got(axs.at[xp], ax_r.at[3])
    az(xp)
    xg_forward(6)
    got(axs.at[x2], ax_r.at[2])
    az(x2)
    xg_forward(7)
    got(bas.at[2 * b + 1 - k], kb_r.at[0])
    g_part(0, 0)
    axg(0)
    xg_rest(0)
    g_part(1, 0)
    axg(1)
    xg_rest(1)
    g_part(2, 0)
    xg_rest(2)
    g_part(3, 0)
    axg_forward(0)

    @pl.loop(0, 8)
    def _(zs):
        got(unit(rb_other, zs), bb_r.at[zs])

    send(bas.at[rb_other], bas.at[rb_other], kb_s.at[1], kb_r.at[1], core_peer)
    axg(2)
    axg_forward(1)
    got(bas.at[2 * (1 - b) + 1 - k], kb_r.at[1])
    for qi in range(4):
        g_part(qi, 1)
    axg(3)
    for qi in range(4):
        g_done(qi, 0)
    g_shared(0)
    axg_forward(2)
    axg_rest(0)
    ob_send(0)
    axg_forward(3)
    axg_rest(1)
    ob_send(1)
    for qi in range(4):
        g_done(qi, 1)
    axg_rest(2)
    ob_send(2)
    axg_rest(3)
    ob_send(3)
    g_shared(1)
    for u in range(4):
        oz(u)

    total = None
    for off in (4, 2, 6, 1, 7, 0):
        zs = (z + off) % 8
        if off:
            got(fin.at[zs], oz_r.at[zs])
        else:
            @pl.when(even == 0)
            def _():
                got(fin.at[z], oz_r.at[z])
        part = fin[zs].astype(F32)
        total = part if total is None else total + part
    out[...] = total

    for d in sent:
        d.wait_send()

    for e in range(4):
        for j in range(2):
            @pl.when(2 * e + j != z)
            def _():
                za_copy(e, j).wait_send()

        @pl.when(2 * e + k != z)
        def _():
            az_copy(e).wait_send()

    for i in range(4):
        for kk in range(2):
            if i < 3:
                oz_copy(i, kk).wait_send()
            else:
                @pl.when(jnp.logical_not(here(i, kk)))
                def _():
                    oz_copy(i, kk).wait_send()


def per_device(acts, grads, act_basis, grad_basis):
    grads = grads.reshape(4, 4, 2, 128, 256)
    V = pltpu.VMEM
    DMA = pltpu.SemaphoreType.DMA
    buffers = [
        V((2, 4, 128, 256), BF16), V((4, 2, 128, 256), BF16), V((4, 128, 2048), BF16), V((4, 2048, 256), BF16),
        V((4, 4, 128, 256), F32), V((4, 4, 128, 256), BF16), V((4, 4, 128, 256), BF16), V((4, 256, 1024), BF16),
        V((4, 1024, 1024), BF16), V((1024, 256), BF16), V((4, 1024, 256), F32), V((2, 1024, 256), F32),
        V((1024, 256), BF16), V((1024, 256), BF16), V((4, 256, 256), BF16), V((4, 256, 256), BF16),
        V((4, 1024, 256), BF16),
        V((4, 2, 256, 256), BF16), V((4, 2, 256, 256), BF16), V((256, 256), F32), V((4, 2, 256, 256), BF16),
        V((8, 256, 256), BF16), V((2, 2, 256, 256), BF16),
    ]
    sems = [DMA((10,)), DMA((4,)), DMA((4,)), DMA((8,)), DMA((8,)), DMA((3, 8)), DMA((3, 8)), DMA((2, 4)), DMA((2, 4)),
            DMA((8,)), DMA((8,)), DMA((2,)), DMA((2,)), DMA((2,)), DMA((2,)), DMA, DMA,
            DMA((4,)), DMA((4,)), DMA((4,)), DMA((4,)), DMA((3, 4)), DMA((3, 4)), DMA((4, 2)), DMA((4, 2)),
            DMA((4, 2)), DMA((4, 2)), DMA((4, 2)), DMA((4, 2)), DMA((4, 2)), DMA((8,)), DMA((2, 2))]
    hbm = pl.BlockSpec(memory_space=pl.ANY)
    return pl.pallas_call(
        kernel,
        out_shape=jax.ShapeDtypeStruct((256, 256), F32),
        in_specs=[hbm] * 4,
        out_specs=pl.BlockSpec(memory_space=pltpu.VMEM),
        scratch_shapes=buffers + sems,
        compiler_params=pltpu.CompilerParams(
            collective_id=0, has_side_effects=True, vmem_limit_bytes=56 * 2**20),
        cost_estimate=pl.CostEstimate(flops=6442450944, bytes_accessed=11534336, transcendentals=0),
    )(acts, grads, act_basis, grad_basis)


def solution(mesh):
    placed = (
        P("grp", None, "row"),
        P("grp", None, "col"),
        P("row", "col"),
        P("col", ("grp", "row")),
    )
    return jax.shard_map(
        per_device, mesh=mesh, in_specs=placed, out_specs=P(("grp", "row"), "col"), check_vma=False
    )
```

```python
import jax
import jax.numpy as jnp
from jax import lax
from jax.experimental import pallas as pl
from jax.experimental.pallas import tpu as pltpu
from jax.sharding import PartitionSpec as P

MESH = pl.DeviceIdType.MESH
F32 = jnp.float32
BF16 = jnp.bfloat16


def kernel(acts, grads, actb, gradb, out, *scratch):
    (gsrc, xs, gq, bas, gp, gs, gr, gt, av, actv, ap, ar, abs_, abr, aown, axs, agat,
     ob, obr, oacc, zsnd, fin, mrg,
     ld, xs_s, xs_r, za_s, za_r, xg_s, xg_r, bz_s, bz_r, bb_s, bb_r, kb_s, kb_r, ak_s, ak_r, ab_s, ab_r,
     ax_s, ax_r, az_s, az_r, axg_s, axg_r, h_s, h_r, gt_s, gt_r, ob_s, ob_r, oz_s, oz_r, mg_r) = scratch
    x = lax.axis_index("grp")
    r = lax.axis_index("row")
    c = lax.axis_index("col")
    b, k, h, z = r // 2, r % 2, c // 8, c % 8
    p = (b + h) % 2
    scale = 1.0 / 16384.0

    def dev(x_, b_, k_, h_, z_):
        return (x_, 2 * b_ + k_, 8 * h_ + z_)

    core_peer = dev(x, b, 1 - k, h, z)
    b_peer = dev(x, 1 - b, k, h, z)
    h_peer = dev(x, 1 - b, k, 1 - h, z)
    xp, xm, x2 = (x + 1) % 4, (x + 3) % 4, (x + 2) % 4
    xp_peer, xm_peer = dev(xp, b, k, h, z), dev(xm, b, k, h, z)
    zp_peer, zm_peer = dev(x, b, k, h, (z + 1) % 8), dev(x, b, k, h, (z + 7) % 8)

    def cp(src, dst, ss, rs, to):
        return pltpu.make_async_remote_copy(
            src_ref=src, dst_ref=dst, send_sem=ss, recv_sem=rs, device_id=to, device_id_type=MESH)

    sent = []

    def send(src, dst, ss, rs, to):
        d = cp(src, dst, ss, rs, to)
        d.start()
        sent.append(d)

    def got(dst, rs):
        cp(dst, dst, ld.at[9], rs, core_peer).wait_recv()

    l_g = pltpu.make_async_copy(grads.at[pl.ds(2 * p, 2), :, k], gsrc, ld.at[0])
    l_x = pltpu.make_async_copy(grads.at[pl.ds(2 * p, 2), x, k], xs.at[x], ld.at[1])
    rb_own = 2 * b + k
    l_b = pltpu.make_async_copy(gradb, bas.at[rb_own, pl.ds(pl.multiple_of(z * 256, 256), 256), :], ld.at[2])
    l_ab = pltpu.make_async_copy(actb, actv, ld.at[3])
    order = (2 * (1 - p) + 1 - k, 2 * (1 - p) + k, 2 * p + 1 - k, 2 * p + k)
    l_a = [pltpu.make_async_copy(acts.at[s], av.at[i], ld.at[4 + i]) for i, s in enumerate(order)]
    for d in [l_g, l_x, l_b, l_ab] + l_a:
        d.start()

    bar = pltpu.get_barrier_semaphore()

    def sig(to):
        pl.semaphore_signal(bar, inc=1, device_id=to, device_id_type=MESH)

    for to in (core_peer, b_peer, h_peer, xp_peer, xm_peer, dev(x2, b, k, h, z)):
        sig(to)

    @pl.loop(1, 8)
    def _(d):
        zt = (z + d) % 8
        sig(dev(x, b, k, h, zt))
        sig(dev(x, b, 1 - k, h, zt))

    pl.semaphore_wait(bar, 20)

    l_g.wait()
    for dx in (1, 3, 2):
        xt = (x + dx) % 4
        send(gsrc.at[:, xt], xs.at[x], xs_s.at[dx], xs_r.at[dx], dev(xt, b, k, h, z))

    def unit(rb, zs):
        return bas.at[rb, pl.ds(pl.multiple_of(zs * 256, 256), 256), :]

    def half(rb, zs, i):
        return bas.at[rb, pl.ds(pl.multiple_of(zs * 256 + 128 * i, 128), 128), :]

    rb_other = 2 * (1 - b) + k

    def b_send(zs):
        send(unit(rb_own, zs), unit(rb_own, zs), bb_s.at[zs], bb_r.at[zs], b_peer)

    def ring(d):
        fwd, bwd = (z - d + 8) % 8, (z + d) % 8
        if d == 0:
            l_b.wait()
            send(unit(rb_own, z), unit(rb_own, z), bz_s.at[0, 0], bz_r.at[0, 0], zp_peer)
            send(unit(rb_own, z), unit(rb_own, z), bz_s.at[1, 0], bz_r.at[1, 0], zm_peer)
        elif d < 3:
            got(unit(rb_own, fwd), bz_r.at[0, d - 1])
            send(unit(rb_own, fwd), unit(rb_own, fwd), bz_s.at[0, d], bz_r.at[0, d], zp_peer)
            got(unit(rb_own, bwd), bz_r.at[1, d - 1])
            send(unit(rb_own, bwd), unit(rb_own, bwd), bz_s.at[1, d], bz_r.at[1, d], zm_peer)
            b_send(fwd)
            b_send(bwd)
        elif d == 3:
            got(unit(rb_own, fwd), bz_r.at[0, 2])
            send(half(rb_own, fwd, 0), half(rb_own, fwd, 0), bz_s.at[0, 3], bz_r.at[0, 3], zp_peer)
            got(unit(rb_own, bwd), bz_r.at[1, 2])
            send(half(rb_own, bwd, 1), half(rb_own, bwd, 1), bz_s.at[1, 3], bz_r.at[1, 3], zm_peer)
            b_send(fwd)
            b_send(bwd)
        else:
            got(half(rb_own, fwd, 0), bz_r.at[0, 3])
            got(half(rb_own, fwd, 1), bz_r.at[1, 3])
            b_send(fwd)
            send(bas.at[rb_own], bas.at[rb_own], kb_s.at[0], kb_r.at[0], core_peer)

    lane = pl.ds(pl.multiple_of(z * 256, 256), 256)

    def za_copy(e, j):
        zt = 2 * e + j
        return cp(xs.at[e, j], gq.at[x, :, lane], za_s.at[zt], za_r.at[(zt + 8 - z) % 8], dev(x, b, k, h, zt))

    def za(e):
        for j in range(2):
            @pl.when(2 * e + j != z)
            def _():
                za_copy(e, j).start()

            @pl.when(2 * e + j == z)
            def _():
                gq[x, :, lane] = xs[e, j]

    pieces = (0, 1, 7, 2, 6, 3, 5, 4)

    def gpiece(q, d):
        zs = (z + 8 - d) % 8
        return gq.at[q, :, pl.ds(pl.multiple_of(zs * 256, 256), 256)]

    def xg(i):
        d = pieces[i]
        if d:
            got(gpiece(x, d), za_r.at[d])
        send(gpiece(x, d), gpiece(x, d), xg_s.at[0, d], xg_r.at[0, d], xp_peer)
        send(gpiece(x, d), gpiece(x, d), xg_s.at[1, d], xg_r.at[1, d], xm_peer)

    def xg_forward(i):
        d = pieces[i]
        if i % 2 == 0:
            got(gpiece(xm, d), xg_r.at[0, d])
            send(gpiece(xm, d), gpiece(xm, d), xg_s.at[2, d], xg_r.at[2, d], xp_peer)
        else:
            got(gpiece(xp, d), xg_r.at[1, d])
            send(gpiece(xp, d), gpiece(xp, d), xg_s.at[2, d], xg_r.at[2, d], xm_peer)

    def xg_rest(side):
        for i, d in enumerate(pieces):
            if side == 2 or i % 2 != side:
                got(gpiece((xm, xp, x2)[side], d), xg_r.at[side, d])

    def a_part(i):
        if i == 0:
            l_ab.wait()
        l_a[i].wait()

        @pl.loop(0, 4)
        def _(m):
            rows = pl.ds(pl.multiple_of(m * 256, 256), 256)
            ap[i, rows, :] = jnp.dot(av[i, rows, :], actv[...], preferred_element_type=F32)

        if i % 2 == 0:
            send(ap.at[i], ar.at[i // 2], ak_s.at[i // 2], ak_r.at[i // 2], core_peer)

    def a_to_b():
        got(ar.at[0], ak_r.at[0])

        @pl.loop(0, 4)
        def _(m):
            rows = pl.ds(pl.multiple_of(m * 256, 256), 256)
            abs_[rows, :] = (ap[1, rows, :] + ar[0, rows, :]).astype(BF16)

        send(abs_, abr, ab_s, ab_r, b_peer)

    def a_sum():
        got(ar.at[1], ak_r.at[1])
        got(abr, ab_r)

        @pl.loop(0, 4)
        def _(m):
            rows = pl.ds(pl.multiple_of(m * 256, 256), 256)
            aown[m] = (ap[3, rows, :] + ar[1, rows, :] + abr[rows, :].astype(F32)).astype(BF16)

        for dx in (1, 3, 2):
            xt = (x + dx) % 4
            send(aown.at[xt], axs.at[x], ax_s.at[dx], ax_r.at[dx], dev(xt, b, k, h, z))
        axs[x] = aown[x]

    quarter = pl.ds(pl.multiple_of(x * 256, 256), 256)

    def az_copy(e):
        return cp(axs.at[e], agat.at[z // 2, quarter, :], az_s.at[e], az_r.at[z // 2], dev(x, b, z % 2, h, 2 * e + k))

    def az(e):
        @pl.when(2 * e + k != z)
        def _():
            az_copy(e).start()

        @pl.when(2 * e + k == z)
        def _():
            agat[z // 2, quarter, :] = axs[e]

    even = 1 - (z + k) % 2
    far = (3 + even, 5 - 3 * even, 1 + 5 * even, 7 - 7 * even)
    units = tuple((z + f) % 8 // 2 for f in far)

    def apiece(q, i):
        return agat.at[units[i], pl.ds(pl.multiple_of(q * 256, 256), 256), :]

    def axg(i):
        @pl.when(2 * units[i] + k != z)
        def _():
            got(apiece(x, i), az_r.at[units[i]])

        send(apiece(x, i), apiece(x, i), axg_s.at[0, i], axg_r.at[0, i], xp_peer)
        send(apiece(x, i), apiece(x, i), axg_s.at[1, i], axg_r.at[1, i], xm_peer)

    def axg_forward(i):
        if i % 2 == 0:
            got(apiece(xm, i), axg_r.at[0, i])
            send(apiece(xm, i), apiece(xm, i), axg_s.at[2, i], axg_r.at[2, i], xp_peer)
        else:
            got(apiece(xp, i), axg_r.at[1, i])
            send(apiece(xp, i), apiece(xp, i), axg_s.at[2, i], axg_r.at[2, i], xm_peer)

    def axg_rest(i):
        if i % 2 == 0:
            got(apiece(xp, i), axg_r.at[1, i])
        else:
            got(apiece(xm, i), axg_r.at[0, i])
        got(apiece(x2, i), axg_r.at[2, i])

    quarters = (x, xm, xp, x2)

    def g_part(qi, i):
        q, bb = quarters[qi], (b, 1 - b)[i]
        for kk in range(2):
            rb = 2 * bb + kk
            part = jnp.dot(gq[q], bas[rb], preferred_element_type=F32)
            gp[q, rb] = part
            gs[q, rb] = part.astype(BF16)
        pair = pl.ds(2 * bb, 2)
        send(gs.at[q, pair], gr.at[q, pair], h_s.at[qi, i], h_r.at[qi, i], h_peer)

    def tok(q, kk):
        return pl.ds(pl.multiple_of(q * 256 + kk * 128, 128), 128)

    def g_done(qi, i):
        q, bb = quarters[qi], (1 - b, b)[i]
        pair = pl.ds(2 * bb, 2)
        got(gr.at[q, pair], h_r.at[qi, i])
        for kk in range(2):
            rb = 2 * bb + kk
            g = (gp[q, rb] + gr[q, rb].astype(F32)).astype(BF16)
            gt[rb, :, tok(q, k)] = g.T
        mine = gt.at[pair, :, tok(q, k)]
        send(mine, mine, gt_s.at[qi, i], gt_r.at[qi, i], core_peer)

    def g_shared(i):
        pair = pl.ds(2 * (1 - b, b)[i], 2)
        for qi in range(4):
            got(gt.at[pair, :, tok(quarters[qi], 1 - k)], gt_r.at[qi, i])

    def tile(rb, u):
        t = jnp.dot(gt[rb], agat[u], preferred_element_type=F32)
        return t * t * scale

    def ob_send(i):
        for kk in range(2):
            ob[i, kk] = tile(2 * (1 - b) + kk, units[i]).astype(BF16)
            send(ob.at[i, kk], obr.at[i, kk], ob_s.at[i, kk], ob_r.at[i, kk], b_peer)

    def oz_copy(i, kk):
        return cp(zsnd.at[i, kk], fin.at[z], oz_s.at[i, kk], oz_r.at[z], dev(x, b, kk, h, (z + far[i]) % 8))

    def merge_copy(i, kk):
        return cp(zsnd.at[i, kk], mrg.at[i, kk], oz_s.at[i, kk], mg_r.at[i, kk], (zp_peer, zm_peer)[i])

    def here(i, kk):
        return jnp.logical_and(even == 1, kk == k)

    def oz(i):
        for kk in range(2):
            oacc[...] = tile(2 * b + kk, units[i])
            got(obr.at[i, kk], ob_r.at[i, kk])
            v = oacc[...] + obr[i, kk].astype(F32)
            zsnd[i, kk] = v.astype(BF16)
            if i in (1, 2):
                oacc[...] = v

                @pl.when(even == 1)
                def _():
                    got(mrg.at[i - 1, kk], mg_r.at[i - 1, kk])
                    zsnd[i, kk] = (oacc[...] + mrg[i - 1, kk].astype(F32)).astype(BF16)

            if i < 2:
                @pl.when(even == 0)
                def _():
                    merge_copy(i, kk).start()

                @pl.when(even == 1)
                def _():
                    oz_copy(i, kk).start()
            elif i == 2:
                oz_copy(i, kk).start()
            else:
                @pl.when(jnp.logical_not(here(i, kk)))
                def _():
                    oz_copy(i, kk).start()

                @pl.when(here(i, kk))
                def _():
                    fin[z] = zsnd[i, kk]

    ring(0)
    l_x.wait()
    za(x)
    a_part(0)
    a_part(1)
    ring(1)
    a_to_b()
    got(xs.at[xm], xs_r.at[1])
    za(xm)
    got(xs.at[xp], xs_r.at[3])
    za(xp)
    got(xs.at[x2], xs_r.at[2])
    za(x2)
    b_send(z)
    xg(0)
    xg(1)
    ring(2)
    xg(2)
    a_part(2)
    xg_forward(0)
    xg(3)
    xg_forward(1)
    a_part(3)
    ring(3)
    xg(4)
    a_sum()
    xg_forward(2)
    xg(5)
    xg_forward(3)
    ring(4)
    xg(6)
    xg_forward(4)
    xg(7)
    xg_forward(5)
    az(x)
    got(axs.at[xm], ax_r.at[1])
    az(xm)
    got(axs.at[xp], ax_r.at[3])
    az(xp)
    xg_forward(6)
    got(axs.at[x2], ax_r.at[2])
    az(x2)
    xg_forward(7)
    got(bas.at[2 * b + 1 - k], kb_r.at[0])
    g_part(0, 0)
    axg(0)
    xg_rest(0)
    g_part(1, 0)
    axg(1)
    xg_rest(1)
    g_part(2, 0)
    xg_rest(2)
    g_part(3, 0)
    axg_forward(0)

    @pl.loop(0, 8)
    def _(zs):
        got(unit(rb_other, zs), bb_r.at[zs])

    send(bas.at[rb_other], bas.at[rb_other], kb_s.at[1], kb_r.at[1], core_peer)
    axg(2)
    axg_forward(1)
    got(bas.at[2 * (1 - b) + 1 - k], kb_r.at[1])
    for qi in range(4):
        g_part(qi, 1)
    axg(3)
    for qi in range(4):
        g_done(qi, 0)
    g_shared(0)
    axg_forward(2)
    axg_rest(0)
    ob_send(0)
    axg_forward(3)
    axg_rest(1)
    ob_send(1)
    for qi in range(4):
        g_done(qi, 1)
    axg_rest(2)
    ob_send(2)
    axg_rest(3)
    ob_send(3)
    g_shared(1)
    for u in range(4):
        oz(u)

    for i, off in enumerate((4, 2, 6, 1, 7, 0)):
        zs = (z + off) % 8
        if off:
            got(fin.at[zs], oz_r.at[zs])
        else:
            @pl.when(even == 0)
            def _():
                got(fin.at[z], oz_r.at[z])
        out[i] = fin[zs]

    for d in sent:
        d.wait_send()

    for e in range(4):
        for j in range(2):
            @pl.when(2 * e + j != z)
            def _():
                za_copy(e, j).wait_send()

        @pl.when(2 * e + k != z)
        def _():
            az_copy(e).wait_send()

    for i in range(4):
        for kk in range(2):
            if i < 3:
                oz_copy(i, kk).wait_send()
            else:
                @pl.when(jnp.logical_not(here(i, kk)))
                def _():
                    oz_copy(i, kk).wait_send()


def per_device(acts, grads, act_basis, grad_basis):
    grads = grads.reshape(4, 4, 2, 128, 256)
    V = pltpu.VMEM
    DMA = pltpu.SemaphoreType.DMA
    buffers = [
        V((2, 4, 128, 256), BF16), V((4, 2, 128, 256), BF16), V((4, 128, 2048), BF16), V((4, 2048, 256), BF16),
        V((4, 4, 128, 256), F32), V((4, 4, 128, 256), BF16), V((4, 4, 128, 256), BF16), V((4, 256, 1024), BF16),
        V((4, 1024, 1024), BF16), V((1024, 256), BF16), V((4, 1024, 256), F32), V((2, 1024, 256), F32),
        V((1024, 256), BF16), V((1024, 256), BF16), V((4, 256, 256), BF16), V((4, 256, 256), BF16),
        V((4, 1024, 256), BF16),
        V((4, 2, 256, 256), BF16), V((4, 2, 256, 256), BF16), V((256, 256), F32), V((4, 2, 256, 256), BF16),
        V((8, 256, 256), BF16), V((2, 2, 256, 256), BF16),
    ]
    sems = [DMA((10,)), DMA((4,)), DMA((4,)), DMA((8,)), DMA((8,)), DMA((3, 8)), DMA((3, 8)), DMA((2, 4)), DMA((2, 4)),
            DMA((8,)), DMA((8,)), DMA((2,)), DMA((2,)), DMA((2,)), DMA((2,)), DMA, DMA,
            DMA((4,)), DMA((4,)), DMA((4,)), DMA((4,)), DMA((3, 4)), DMA((3, 4)), DMA((4, 2)), DMA((4, 2)),
            DMA((4, 2)), DMA((4, 2)), DMA((4, 2)), DMA((4, 2)), DMA((4, 2)), DMA((8,)), DMA((2, 2))]
    hbm = pl.BlockSpec(memory_space=pl.ANY)
    parts = pl.pallas_call(
        kernel,
        out_shape=jax.ShapeDtypeStruct((6, 256, 256), BF16),
        in_specs=[hbm] * 4,
        out_specs=pl.BlockSpec(memory_space=pltpu.VMEM),
        scratch_shapes=buffers + sems,
        compiler_params=pltpu.CompilerParams(
            collective_id=0, has_side_effects=True, vmem_limit_bytes=56 * 2**20),
        cost_estimate=pl.CostEstimate(flops=6442450944, bytes_accessed=11534336, transcendentals=0),
    )(acts, grads, act_basis, grad_basis)
    return jnp.sum(parts.astype(F32), axis=0)


def solution(mesh):
    placed = (
        P("grp", None, "row"),
        P("grp", None, "col"),
        P("row", "col"),
        P("col", ("grp", "row")),
    )
    return jax.shard_map(
        per_device, mesh=mesh, in_specs=placed, out_specs=P(("grp", "row"), "col"), check_vma=False
    )
```
